128 devices in a mesh: mu: 8 (over z, core), nu: 16 (over x, y).
Axes of the slice: x: 4, y: 4, z: 4, core: 2. Of those that a mesh axis runs over, the one named last changes fastest.
Arguments:
- integrals: bfloat16 [2, 10240, 10240], P(None, 'mu', 'nu'), may hold values from -6 to 6
- block_mask: int32 [160, 160], P('mu', 'nu'), may hold values 0 or 1
- occ_coef: bfloat16 [10240, 2048], P('mu', 'nu'), may hold values from -0.078125 to 0.078125
- virt_coef: bfloat16 [10240, 8192], P(None, 'mu'), may hold values from -0.0625 to 0.0625
Outputs:
- pair_ints: bfloat16 [2048, 2, 8192], P('nu', None, 'mu')
The draws below stay inside these ranges and needn't reach their ends.
All inputs are finite; a program needn't handle non-finite values. No bound on the sum of `block_mask` on one device may be relied on, other than what follows from the above.
Results may differ from the reference program's by a relative error of at most 0.02.
Values may be sent and summed in bfloat16 or wider, within the bound.
A program may use at most 128 MiB of HBM per device.

```python
import jax
import jax.numpy as jnp
from jax import lax

NB = 10240
OCC = 2048
VIRT = 8192
AUX = 2
BLK = 64
NBLK = 160


def with_ends(array, stream_key, low, high):
    spot = [jax.random.randint(jax.random.fold_in(stream_key, axis), (), 0, length) for axis, length in enumerate(array.shape)]
    widest = array.shape.index(max(array.shape))
    beside = spot[:widest] + [(spot[widest] + 1) % array.shape[widest]] + spot[widest + 1:]
    return array.at[tuple(spot)].set(low).at[tuple(beside)].set(high)


def steps_of(rng, dims, shards, least, largest):
    gain = 1.0
    for position, shards_of in shards:
        steps = jax.random.uniform(jax.random.fold_in(jax.random.fold_in(rng, 6), position), (shards_of,), jnp.float32, least / len(shards), largest / len(shards))
        gain = gain * jnp.repeat(jnp.exp(steps), dims[position] // shards_of).reshape((-1,) + (1,) * (len(dims) - 1 - position))
    return gain


def noise(own_key, extent, deviation, bound, split=(), kind=jnp.bfloat16):
    values = jax.random.normal(own_key, extent, jnp.float32) * deviation
    if len(split) > 0:
        values = steps_of(own_key, extent, split, -0.22, 0.18) * values
    return jnp.clip(values, min=-bound, max=bound).astype(kind)


def setup_inputs(seed: int = 0) -> dict:
    splits = jax.random.split(jax.random.key(seed), 5)
    return {
        "integrals": noise(splits[0], (AUX, NB, NB), 1.0, 6.0, ((1, 8), (2, 16))),
        "block_mask": with_ends((jax.random.randint(splits[1], (NBLK, NBLK), 0, 2) < 1).astype(jnp.int32), jax.random.fold_in(splits[1], 1), 0, 1),
        "occ_coef": noise(splits[2], (NB, OCC), (NB // 2) ** -0.5, 0.078125, ((0, 8), (1, 16))),
        "virt_coef": noise(splits[3], (NB, VIRT), NB ** -0.5, 0.0625, ((1, 8),)),
    }


def reference(integrals, block_mask, occ_coef, virt_coef):
    full_mask = jnp.repeat(jnp.repeat(block_mask, BLK, axis=0), BLK, axis=1).astype(jnp.bfloat16)
    occ_left = occ_coef.T

    def one_aux(slab):
        masked = slab * full_mask
        half = jnp.dot(occ_left, masked, preferred_element_type=jnp.float32).astype(jnp.bfloat16)
        return jnp.dot(half, virt_coef, preferred_element_type=jnp.float32).astype(jnp.bfloat16)

    result = lax.map(one_aux, integrals)
    return jnp.transpose(result, (1, 0, 2))
```

```python
import functools

import jax
import jax.numpy as jnp
from jax import lax
from jax.experimental import pallas as pl
from jax.experimental.pallas import tpu as pltpu
from jax.sharding import PartitionSpec as P

MESH = pl.DeviceIdType.MESH
BLK = 64
F32, BF16 = jnp.float32, jnp.bfloat16

ORDER = [
    ("A", 0, 0), ("B", 0, 0),
    ("A", 1, 0), ("A", -1, 0),
    ("B", 0, -1), ("B", 0, 1),
    ("A", 0, -1), ("A", 0, 1),
    ("B", -1, 0), ("B", 1, 0),
    ("A", 2, 0), ("A", 1, -1),
    ("A", 1, 1), ("B", -1, -1),
    ("A", -1, -1), ("A", -1, 1),
    ("B", 1, -1), ("B", -1, 1),
    ("B", 0, 2), ("B", 1, 1),
    ("A", 0, 2), ("B", 2, -1),
    ("B", 2, 0), ("A", 2, -1),
    ("A", 2, 1), ("B", -1, 2),
    ("A", 1, 2), ("A", -1, 2),
    ("B", 1, 2), ("B", 2, 2),
    ("B", 2, 1), ("A", 2, 2),
]
SLOT = {key: divmod(n, 2) for n, key in enumerate(ORDER)}
UNITS = 16
LAG = dict(gather=0, product=0, pair=1, ring1=2, ring2=3, spread=5, relay=6, sibling=7, final=8)
STEPS = {"x+": (1, 0), "x-": (-1, 0), "y+": (0, 1), "y-": (0, -1)}


def forwards(half, dx, dy):
    out = []
    if half == "A":
        if dy == 0:
            if dx == 0:
                out += [("x-", ("A", 1, 0)), ("x+", ("A", -1, 0))]
            out += [("y+", ("A", dx, -1)), ("y-", ("A", dx, 1))]
            if dx == 1:
                out += [("x-", ("A", 2, 0))]
        elif dy == 1 and dx in (0, 1):
            out += [("y-", ("A", dx, 2))]
        elif dy == -1 and dx in (-1, 2):
            out += [("y+", ("A", dx, 2))]
    else:
        if dx == 0:
            if dy == 0:
                out += [("y+", ("B", 0, -1)), ("y-", ("B", 0, 1))]
            out += [("x+", ("B", -1, dy)), ("x-", ("B", 1, dy))]
            if dy == -1:
                out += [("y+", ("B", 0, 2))]
        elif dx == 1 and dy in (0, 1):
            out += [("x-", ("B", 2, dy))]
        elif dx == -1 and dy in (-1, 2):
            out += [("x+", ("B", 2, dy))]
    return out


def kernel(
    ints_hbm, mask_ref, occ_ref, virt_hbm, out_ref,
    masked, virt, occ, part, xr, sums, r1, s2, r2, fin, half, acc, mrow,
    load_sem, virt_sem, occ_send, occ_recv, x_send, x_recv, r1_send, r1_recv, r2_send, r2_recv,
    a_send, a_recv, g1_send, g1_recv, g2_send, g2_recv, s_send, s_recv,
):
    mu, nu = lax.axis_index("mu"), lax.axis_index("nu")
    x, y, z, c = nu // 4, nu % 4, mu // 2, mu % 2
    rows, cols = ints_hbm.shape[1:]

    def at(dx=0, dy=0, dz=0, dc=0):
        return {
            "mu": ((z + dz + 4) % 4) * 2 + (c + dc) % 2,
            "nu": ((x + dx + 4) % 4) * 4 + (y + dy + 4) % 4,
        }

    def send(src, dst, send_sem, recv_sem, to):
        pltpu.make_async_remote_copy(
            src_ref=src, dst_ref=dst, send_sem=send_sem, recv_sem=recv_sem, device_id=to, device_id_type=MESH
        ).start()

    def wait(ref, sem):
        pltpu.make_async_copy(ref, ref, sem).wait()

    loads = [
        pltpu.make_async_copy(ints_hbm.at[p], masked.at[:, pl.ds(p * cols, cols)], load_sem.at[p])
        for p in range(2)
    ]
    for load in loads:
        load.start()

    barrier = pltpu.get_barrier_semaphore()
    greet = [at(dx, dy) for dx in range(-1, 3) for dy in range(-1, 3) if (dx, dy) != (0, 0)]
    greet += [at(dz=1), at(dz=-1), at(dc=1)]
    for to in greet:
        pl.semaphore_signal(barrier, inc=1, device_id=to, device_id_type=MESH)

    occ[0] = occ_ref[...].T.reshape(2, BLK, rows)
    pl.semaphore_wait(barrier, len(greet))

    def occ_send_to(key, link, their):
        (u, h), (tu, th) = SLOT[key], SLOT[their]
        send(occ.at[u, h], occ.at[tu, th], occ_send, occ_recv.at[tu, th], at(*STEPS[link]))

    for link, key, their in [
        ("x-", ("A", 0, 0), ("A", 1, 0)), ("x+", ("A", 0, 0), ("A", -1, 0)),
        ("y+", ("B", 0, 0), ("B", 0, -1)), ("y-", ("B", 0, 0), ("B", 0, 1)),
        ("y+", ("A", 0, 0), ("A", 0, -1)), ("y-", ("A", 0, 0), ("A", 0, 1)),
        ("x+", ("B", 0, 0), ("B", -1, 0)), ("x-", ("B", 0, 0), ("B", 1, 0)),
    ]:
        occ_send_to(key, link, their)

    lane_block = lax.broadcasted_iota(jnp.int32, (mask_ref.shape[0], 2 * cols), 1) % cols // BLK
    spread_mask = jnp.zeros((mask_ref.shape[0], 2 * cols), F32)
    blocks = mask_ref[...].astype(F32)
    for b in range(mask_ref.shape[1]):
        spread_mask = jnp.where(lane_block == b, blocks[:, b : b + 1], spread_mask)
    mrow[...] = spread_mask
    for load in loads:
        load.wait()
    virt_load = pltpu.make_async_copy(virt_hbm, virt, virt_sem)
    virt_load.start()
    for r in range(mask_ref.shape[0]):
        keep = mrow[r : r + 1, :].astype(BF16)
        masked[r * BLK : (r + 1) * BLK, :] = masked[r * BLK : (r + 1) * BLK, :] * keep
    acc[...] = jnp.zeros_like(acc)

    mine = pl.ds(pl.multiple_of(c * cols, 128), cols)
    theirs = pl.ds(pl.multiple_of((1 - c) * cols, 128), cols)

    def zrows(dz):
        return pl.ds(pl.multiple_of(((z + dz + 4) % 4) * 16, 16), 16)

    def hrows(dz):
        return pl.ds(pl.multiple_of(c * BLK + ((z + dz + 4) % 4) * 16, 16), 16)

    def gather(u):
        for h in range(2):
            key = ORDER[2 * u + h]
            wait(occ.at[u, h], occ_recv.at[u, h])
            for link, their in forwards(*key):
                occ_send_to(key, link, their)

    def product(u):
        left = occ[u].reshape(2 * BLK, rows)
        for j in range(0, 2 * cols, 256):
            tile = jnp.dot(left, masked[:, j : j + 256], preferred_element_type=F32)
            part[u, :, :, j : j + 256] = tile.astype(BF16).reshape(2, BLK, 256)
        send(part.at[u, :, :, theirs], xr.at[u], x_send, x_recv.at[u], at(dc=1))

    def pair(u):
        wait(xr.at[u], x_recv.at[u])
        sums[u] = (part[u, :, :, mine].astype(F32) + xr[u].astype(F32)).astype(BF16)
        send(sums.at[u, 0, zrows(2)], r1.at[u, 0], r1_send, r1_recv.at[u, 0], at(dz=1))
        send(sums.at[u, 1, zrows(2)], r1.at[u, 1], r1_send, r1_recv.at[u, 1], at(dz=-1))
        send(sums.at[u, 1, zrows(1)], r2.at[u, 0, 1], r2_send, r2_recv.at[u, 0], at(dz=1))
        send(sums.at[u, 0, zrows(-1)], r2.at[u, 1, 0], r2_send, r2_recv.at[u, 1], at(dz=-1))

    def ring1(u):
        for side, dz in ((0, 1), (1, -1)):
            wait(r1.at[u, side], r1_recv.at[u, side])
            own = sums[u, side, zrows(dz)].astype(F32)
            s2[u, side] = (own + r1[u, side].astype(F32)).astype(BF16)
            send(s2.at[u, side], r2.at[u, side, side], r2_send, r2_recv.at[u, side], at(dz=dz))

    def ring2(u):
        for side in range(2):
            wait(r2.at[u, side], r2_recv.at[u, side])
        total = sums[u, :, zrows(0)].astype(F32) + r2[u, 0].astype(F32) + r2[u, 1].astype(F32)
        if u == 0:
            half[0, :, hrows(0)] = total.astype(BF16)
            return
        fin[u] = total.astype(BF16)
        for h in range(2):
            _, dx, dy = ORDER[2 * u + h]
            send(fin.at[u, h], half.at[u, h, hrows(0)], a_send, a_recv.at[u], at(dx, dy))

    def spread(u):
        here = half.at[u, :, hrows(0)]
        if u > 0:
            wait(here, a_recv.at[u])
        send(here, here, g1_send, g1_recv.at[u, 0], at(dz=1))
        send(here, here, g1_send, g1_recv.at[u, 1], at(dz=-1))
        send(here, here, s_send, s_recv.at[u], at(dc=1))

    def relay(u):
        for side, dz in ((0, 1), (1, -1)):
            came = half.at[u, :, hrows(-dz)]
            wait(came, g1_recv.at[u, side])
            on = half.at[u, side, hrows(-dz)]
            send(on, on, g2_send, g2_recv.at[u, side], at(dz=dz))
            send(came, came, s_send, s_recv.at[u], at(dc=1))

    def sibling(u):
        for side in range(2):
            wait(half.at[u, side, hrows(2)], g2_recv.at[u, side])
        came = half.at[u, :, hrows(2)]
        send(came, came, s_send, s_recv.at[u], at(dc=1))

    def final(u):
        other = pl.ds(pl.multiple_of((1 - c) * BLK, 16), BLK)
        wait(half.at[u, :, other], s_recv.at[u])
        for h in range(2):
            kind, dx, dy = ORDER[2 * u + h]
            (ua, ha), (ub, hb) = SLOT["A", dx, dy], SLOT["B", dx, dy]
            if (u, h) != max((ua, ha), (ub, hb)):
                continue
            left = jnp.concatenate([half[ua, ha], half[ub, hb]], axis=0)
            n_block = ((x - dx + 4) % 4) * 4 + (y - dy + 4) % 4
            deep = pl.ds(pl.multiple_of(n_block * cols, cols), cols)
            for j in range(0, virt.shape[1], 256):
                acc[:, j : j + 256] += jnp.dot(left, virt[deep, j : j + 256], preferred_element_type=F32)

    stages = dict(
        final=final, sibling=sibling, relay=relay, spread=spread, ring2=ring2, ring1=ring1, pair=pair,
        gather=gather, product=product,
    )
    for t in range(UNITS + max(LAG.values())):
        for name, stage in stages.items():
            u = t - LAG[name]
            if 0 <= u < UNITS and not (name == "gather" and u == 0):
                if name == "final" and u == 0:
                    virt_load.wait()
                stage(u)

    out_ref[...] = acc[...].astype(BF16)
    wait(occ.at[pl.ds(1, UNITS - 1)], occ_send)
    wait(xr, x_send)
    wait(r1, r1_send)
    wait(r2, r2_send)
    wait(fin.at[pl.ds(1, UNITS - 1)], a_send)
    wait(r2, g1_send)
    wait(r1, g2_send)
    wait(xr, s_send)


def shards(integrals, block_mask, occ_coef, virt_coef):
    _, rows, cols = integrals.shape
    own, virt_cols = occ_coef.shape[1], virt_coef.shape[1]
    assert own == 2 * BLK
    vmem, dma = pltpu.VMEM, pltpu.SemaphoreType.DMA
    result = pl.pallas_call(
        kernel,
        name="transform",
        out_shape=jax.ShapeDtypeStruct((2 * own, virt_cols), BF16),
        in_specs=[
            pl.BlockSpec(memory_space=pl.ANY),
            pl.BlockSpec(memory_space=pltpu.VMEM),
            pl.BlockSpec(memory_space=pltpu.VMEM),
            pl.BlockSpec(memory_space=pl.ANY),
        ],
        out_specs=pl.BlockSpec(memory_space=pltpu.VMEM),
        scratch_shapes=[
            vmem((rows, 2 * cols), BF16),
            vmem(virt_coef.shape, BF16),
            vmem((UNITS, 2, BLK, rows), BF16),
            vmem((UNITS, 2, BLK, 2 * cols), BF16),
            vmem((UNITS, 2, BLK, cols), BF16),
            vmem((UNITS, 2, BLK, cols), BF16),
            vmem((UNITS, 2, 16, cols), BF16),
            vmem((UNITS, 2, 16, cols), BF16),
            vmem((UNITS, 2, 2, 16, cols), BF16),
            vmem((UNITS, 2, 16, cols), BF16),
            vmem((UNITS, 2, 2 * BLK, cols), BF16),
            vmem((2 * own, virt_cols), F32),
            vmem((block_mask.shape[0], 2 * cols), F32),
            dma((2,)), dma,
            dma, dma((UNITS, 2)),
            dma, dma((UNITS,)),
            dma, dma((UNITS, 2)),
            dma, dma((UNITS, 2)),
            dma, dma((UNITS,)),
            dma, dma((UNITS, 2)),
            dma, dma((UNITS, 2)),
            dma, dma((UNITS,)),
        ],
        compiler_params=pltpu.CompilerParams(
            collective_id=0, has_side_effects=True, vmem_limit_bytes=62 * 2**20
        ),
    )(integrals, block_mask, occ_coef, virt_coef)
    result = result.reshape(2, 2, BLK, virt_cols).transpose(0, 2, 1, 3)
    return result.reshape(own, 2, virt_cols)


def solution(mesh):
    return jax.shard_map(
        shards,
        mesh=mesh,
        in_specs=(P(None, "mu", "nu"), P("mu", "nu"), P("mu", "nu"), P(None, "mu")),
        out_specs=P("nu", None, "mu"),
        check_vma=False,
    )
```

```python
import functools

import jax
import jax.numpy as jnp
from jax import lax
from jax.experimental import pallas as pl
from jax.experimental.pallas import tpu as pltpu
from jax.sharding import PartitionSpec as P

MESH = pl.DeviceIdType.MESH
BLK = 64
F32, BF16 = jnp.float32, jnp.bfloat16

ORDER = [
    ("A", 0, 0), ("B", 0, 0),
    ("A", 1, 0), ("A", -1, 0),
    ("B", 0, -1), ("B", 0, 1),
    ("A", 0, -1), ("A", 0, 1),
    ("B", -1, 0), ("B", 1, 0),
    ("A", 2, 0), ("A", 1, -1),
    ("A", 1, 1), ("B", -1, -1),
    ("A", -1, -1), ("A", -1, 1),
    ("B", 1, -1), ("B", -1, 1),
    ("B", 0, 2), ("B", 1, 1),
    ("A", 0, 2), ("B", 2, -1),
    ("B", 2, 0), ("A", 2, -1),
    ("A", 2, 1), ("B", -1, 2),
    ("A", 1, 2), ("A", -1, 2),
    ("B", 1, 2), ("B", 2, 2),
    ("B", 2, 1), ("A", 2, 2),
]
SLOT = {key: divmod(n, 2) for n, key in enumerate(ORDER)}
UNITS = 16
CHUNKS = 4
STAGES = ("gather", "product", "pair", "ring1", "ring2", "spread", "relay", "sibling", "final")
STEPS = [
    32, 64, 2, 3, 33, 4, 5, 34, 96, 66, 9, 65, 7, 6, 35, 8, 128, 160, 36, 98,
    67, 97, 10, 13, 11, 37, 69, 68, 130, 12, 38, 99, 129, 17, 16, 40, 192, 14, 15, 70,
    39, 72, 71, 101, 100, 19, 18, 41, 102, 20, 21, 42, 104, 73, 74, 103, 224, 22, 133, 23,
    43, 24, 161, 162, 75, 25, 44, 105, 106, 26, 193, 76, 27, 132, 131, 30, 134, 165, 45, 107,
    194, 77, 31, 47, 28, 135, 108, 138, 163, 137, 29, 46, 79, 78, 139, 109, 166, 164, 195, 110,
    136, 111, 226, 167, 169, 141, 170, 140, 196, 142, 198, 258, 143, 227, 168, 199, 225, 201, 257, 173,
    256, 171, 202, 228, 172, 197, 230, 260, 233, 231, 174, 262, 200, 175, 263, 265, 203, 234, 205, 259,
    229, 204, 206, 261, 266, 232, 207, 235, 264, 237, 236, 238, 267, 268, 239, 269, 270, 271,
]
LINKS = {"x+": (1, 0), "x-": (-1, 0), "y+": (0, 1), "y-": (0, -1)}


def forwards(half, dx, dy):
    out = []
    if half == "A":
        if dy == 0:
            if dx == 0:
                out += [("x-", ("A", 1, 0)), ("x+", ("A", -1, 0))]
            out += [("y+", ("A", dx, -1)), ("y-", ("A", dx, 1))]
            if dx == 1:
                out += [("x-", ("A", 2, 0))]
        elif dy == 1 and dx in (0, 1):
            out += [("y-", ("A", dx, 2))]
        elif dy == -1 and dx in (-1, 2):
            out += [("y+", ("A", dx, 2))]
    else:
        if dx == 0:
            if dy == 0:
                out += [("y+", ("B", 0, -1)), ("y-", ("B", 0, 1))]
            out += [("x+", ("B", -1, dy)), ("x-", ("B", 1, dy))]
            if dy == -1:
                out += [("y+", ("B", 0, 2))]
        elif dx == 1 and dy in (0, 1):
            out += [("x-", ("B", 2, dy))]
        elif dx == -1 and dy in (-1, 2):
            out += [("x+", ("B", 2, dy))]
    return out


def kernel(
    ints_hbm, mask_hbm, occ_hbm, virt_hbm, out_ref,
    masked, virt, occ, part, xr, sums, r1, s2, r2, fin, half, acc, mrow, mask_ref, occ_ref,
    load_sem, small_sem, virt_sem, occ_send, occ_recv, x_send, x_recv, r1_send, r1_recv, r2_send, r2_recv,
    a_send, a_recv, g1_send, g1_recv, g2_send, g2_recv, s_send, s_recv,
):
    mu, nu = lax.axis_index("mu"), lax.axis_index("nu")
    x, y, z, c = nu // 4, nu % 4, mu // 2, mu % 2
    rows, cols = ints_hbm.shape[1:]

    def at(dx=0, dy=0, dz=0, dc=0):
        return {
            "mu": ((z + dz + 4) % 4) * 2 + (c + dc) % 2,
            "nu": ((x + dx + 4) % 4) * 4 + (y + dy + 4) % 4,
        }

    def send(src, dst, send_sem, recv_sem, to):
        pltpu.make_async_remote_copy(
            src_ref=src, dst_ref=dst, send_sem=send_sem, recv_sem=recv_sem, device_id=to, device_id_type=MESH
        ).start()

    def wait(ref, sem):
        pltpu.make_async_copy(ref, ref, sem).wait()

    small = [
        pltpu.make_async_copy(occ_hbm, occ_ref, small_sem.at[0]),
        pltpu.make_async_copy(mask_hbm, mask_ref, small_sem.at[1]),
    ]
    chunk = rows // CHUNKS
    loads = [
        pltpu.make_async_copy(
            ints_hbm.at[p, pl.ds(q * chunk, chunk)],
            masked.at[pl.ds(q * chunk, chunk), pl.ds(p * cols, cols)],
            load_sem.at[q, p],
        )
        for q in range(CHUNKS)
        for p in range(2)
    ]

    barrier = pltpu.get_barrier_semaphore()
    greet = [at(dx, dy) for dx in range(-1, 3) for dy in range(-1, 3) if (dx, dy) != (0, 0)]
    greet += [at(dz=1), at(dz=-1), at(dc=1)]
    for to in greet:
        pl.semaphore_signal(barrier, inc=1, device_id=to, device_id_type=MESH)
    for load in small + loads:
        load.start()

    small[0].wait()
    occ[0] = occ_ref[...].T.reshape(2, BLK, rows)
    small[1].wait()
    n_blocks, m_blocks = mask_ref.shape
    lane_block = lax.broadcasted_iota(jnp.int32, (n_blocks, 2 * cols), 1) % cols // BLK
    pick = lane_block == lax.broadcasted_iota(jnp.int32, lane_block.shape, 0)
    mrow[...] = lax.dot_general(
        mask_ref[...].astype(BF16), pick.astype(BF16), (((0,), (0,)), ((), ())), preferred_element_type=F32
    )
    acc[...] = jnp.zeros_like(acc)
    pl.semaphore_wait(barrier, len(greet))

    def occ_send_to(key, link, their):
        (u, h), (tu, th) = SLOT[key], SLOT[their]
        send(occ.at[u, h], occ.at[tu, th], occ_send, occ_recv.at[tu, th], at(*LINKS[link]))

    for link, key, their in [
        ("x-", ("A", 0, 0), ("A", 1, 0)), ("x+", ("A", 0, 0), ("A", -1, 0)),
        ("y+", ("B", 0, 0), ("B", 0, -1)), ("y-", ("B", 0, 0), ("B", 0, 1)),
        ("y+", ("A", 0, 0), ("A", 0, -1)), ("y-", ("A", 0, 0), ("A", 0, 1)),
        ("x+", ("B", 0, 0), ("B", -1, 0)), ("x-", ("B", 0, 0), ("B", 1, 0)),
    ]:
        occ_send_to(key, link, their)

    virt_load = pltpu.make_async_copy(virt_hbm, virt, virt_sem)
    virt_load.start()
    per = chunk // BLK
    for q in range(CHUNKS):
        for load in loads[2 * q : 2 * q + 2]:
            load.wait()
        for r in range(q * per, (q + 1) * per):
            keep = mrow[r : r + 1, :].astype(BF16)
            masked[r * BLK : (r + 1) * BLK, :] = masked[r * BLK : (r + 1) * BLK, :] * keep

    mine = pl.ds(pl.multiple_of(c * cols, 128), cols)
    theirs = pl.ds(pl.multiple_of((1 - c) * cols, 128), cols)

    def zrows(dz):
        return pl.ds(pl.multiple_of(((z + dz + 4) % 4) * 16, 16), 16)

    def hrows(dz):
        return pl.ds(pl.multiple_of(c * BLK + ((z + dz + 4) % 4) * 16, 16), 16)

    def gather(n):
        u, h = divmod(n, 2)
        wait(occ.at[u, h], occ_recv.at[u, h])
        for link, their in forwards(*ORDER[n]):
            occ_send_to(ORDER[n], link, their)

    def product(u):
        left = occ[u].reshape(2 * BLK, rows)
        for j in range(0, 2 * cols, 256):
            tile = jnp.dot(left, masked[:, j : j + 256], preferred_element_type=F32)
            part[u, :, :, j : j + 256] = tile.astype(BF16).reshape(2, BLK, 256)
        send(part.at[u, :, :, theirs], xr.at[u], x_send, x_recv.at[u], at(dc=1))

    def pair(u):
        wait(xr.at[u], x_recv.at[u])
        sums[u] = (part[u, :, :, mine].astype(F32) + xr[u].astype(F32)).astype(BF16)
        send(sums.at[u, 0, zrows(2)], r1.at[u, 0], r1_send, r1_recv.at[u, 0], at(dz=1))
        send(sums.at[u, 1, zrows(2)], r1.at[u, 1], r1_send, r1_recv.at[u, 1], at(dz=-1))
        send(sums.at[u, 1, zrows(1)], r2.at[u, 0, 1], r2_send, r2_recv.at[u, 0], at(dz=1))
        send(sums.at[u, 0, zrows(-1)], r2.at[u, 1, 0], r2_send, r2_recv.at[u, 1], at(dz=-1))

    def ring1(u):
        for side, dz in ((0, 1), (1, -1)):
            wait(r1.at[u, side], r1_recv.at[u, side])
            own = sums[u, side, zrows(dz)].astype(F32)
            s2[u, side] = (own + r1[u, side].astype(F32)).astype(BF16)
            send(s2.at[u, side], r2.at[u, side, side], r2_send, r2_recv.at[u, side], at(dz=dz))

    def ring2(u):
        for side in range(2):
            wait(r2.at[u, side], r2_recv.at[u, side])
        total = sums[u, :, zrows(0)].astype(F32) + r2[u, 0].astype(F32) + r2[u, 1].astype(F32)
        if u == 0:
            half[0, :, hrows(0)] = total.astype(BF16)
            return
        fin[u] = total.astype(BF16)
        for h in range(2):
            _, dx, dy = ORDER[2 * u + h]
            send(fin.at[u, h], half.at[u, h, hrows(0)], a_send, a_recv.at[u], at(dx, dy))

    def spread(u):
        here = half.at[u, :, hrows(0)]
        if u > 0:
            wait(here, a_recv.at[u])
        send(here, here, g1_send, g1_recv.at[u, 0], at(dz=1))
        send(here, here, g1_send, g1_recv.at[u, 1], at(dz=-1))
        send(here, here, s_send, s_recv.at[u], at(dc=1))

    def relay(u):
        for side, dz in ((0, 1), (1, -1)):
            came = half.at[u, :, hrows(-dz)]
            wait(came, g1_recv.at[u, side])
            on = half.at[u, side, hrows(-dz)]
            send(on, on, g2_send, g2_recv.at[u, side], at(dz=dz))
            send(came, came, s_send, s_recv.at[u], at(dc=1))

    def sibling(u):
        for side in range(2):
            wait(half.at[u, side, hrows(2)], g2_recv.at[u, side])
        came = half.at[u, :, hrows(2)]
        send(came, came, s_send, s_recv.at[u], at(dc=1))

    def final(u):
        other = pl.ds(pl.multiple_of((1 - c) * BLK, 16), BLK)
        wait(half.at[u, :, other], s_recv.at[u])
        for h in range(2):
            kind, dx, dy = ORDER[2 * u + h]
            (ua, ha), (ub, hb) = SLOT["A", dx, dy], SLOT["B", dx, dy]
            if (u, h) != max((ua, ha), (ub, hb)):
                continue
            left = jnp.concatenate([half[ua, ha], half[ub, hb]], axis=0)
            n_block = ((x - dx + 4) % 4) * 4 + (y - dy + 4) % 4
            deep = pl.ds(pl.multiple_of(n_block * cols, cols), cols)
            for j in range(0, virt.shape[1], 256):
                acc[:, j : j + 256] += jnp.dot(left, virt[deep, j : j + 256], preferred_element_type=F32)

    stages = (gather, product, pair, ring1, ring2, spread, relay, sibling, final)
    need_virt = True
    for step in STEPS:
        stage, n = divmod(step, 32)
        if need_virt and STAGES[stage] == "final":
            virt_load.wait()
            need_virt = False
        stages[stage](n)

    out_ref[...] = acc[...].astype(BF16)
    wait(occ.at[pl.ds(1, UNITS - 1)], occ_send)
    wait(xr, x_send)
    wait(r1, r1_send)
    wait(r2, r2_send)
    wait(fin.at[pl.ds(1, UNITS - 1)], a_send)
    wait(r2, g1_send)
    wait(r1, g2_send)
    wait(xr, s_send)


def shards(integrals, block_mask, occ_coef, virt_coef):
    _, rows, cols = integrals.shape
    own, virt_cols = occ_coef.shape[1], virt_coef.shape[1]
    assert own == 2 * BLK
    vmem, dma = pltpu.VMEM, pltpu.SemaphoreType.DMA
    result = pl.pallas_call(
        kernel,
        name="transform",
        out_shape=jax.ShapeDtypeStruct((2 * own, virt_cols), BF16),
        in_specs=[
            pl.BlockSpec(memory_space=pl.ANY),
            pl.BlockSpec(memory_space=pl.ANY),
            pl.BlockSpec(memory_space=pl.ANY),
            pl.BlockSpec(memory_space=pl.ANY),
        ],
        out_specs=pl.BlockSpec(memory_space=pltpu.VMEM),
        scratch_shapes=[
            vmem((rows, 2 * cols), BF16),
            vmem(virt_coef.shape, BF16),
            vmem((UNITS, 2, BLK, rows), BF16),
            vmem((UNITS, 2, BLK, 2 * cols), BF16),
            vmem((UNITS, 2, BLK, cols), BF16),
            vmem((UNITS, 2, BLK, cols), BF16),
            vmem((UNITS, 2, 16, cols), BF16),
            vmem((UNITS, 2, 16, cols), BF16),
            vmem((UNITS, 2, 2, 16, cols), BF16),
            vmem((UNITS, 2, 16, cols), BF16),
            vmem((UNITS, 2, 2 * BLK, cols), BF16),
            vmem((2 * own, virt_cols), F32),
            vmem((block_mask.shape[0], 2 * cols), F32),
            vmem(block_mask.shape[::-1], jnp.int32),
            vmem(occ_coef.shape, BF16),
            dma((CHUNKS, 2)), dma((2,)), dma,
            dma, dma((UNITS, 2)),
            dma, dma((UNITS,)),
            dma, dma((UNITS, 2)),
            dma, dma((UNITS, 2)),
            dma, dma((UNITS,)),
            dma, dma((UNITS, 2)),
            dma, dma((UNITS, 2)),
            dma, dma((UNITS,)),
        ],
        compiler_params=pltpu.CompilerParams(
            collective_id=0, has_side_effects=True, vmem_limit_bytes=62 * 2**20
        ),
    )(integrals, block_mask.T, occ_coef, virt_coef)
    result = result.reshape(2, 2, BLK, virt_cols).transpose(0, 2, 1, 3)
    return result.reshape(own, 2, virt_cols)


def solution(mesh):
    return jax.shard_map(
        shards,
        mesh=mesh,
        in_specs=(P(None, "mu", "nu"), P("mu", "nu"), P("mu", "nu"), P(None, "mu")),
        out_specs=P("nu", None, "mu"),
        check_vma=False,
    )
```

```python
import functools

import jax
import jax.numpy as jnp
from jax import lax
from jax.experimental import pallas as pl
from jax.experimental.pallas import tpu as pltpu
from jax.sharding import PartitionSpec as P

MESH = pl.DeviceIdType.MESH
BLK = 64
F32, BF16 = jnp.float32, jnp.bfloat16

ORDER = [
    ("A", 0, 0), ("B", 0, 0),
    ("A", 1, 0), ("A", -1, 0),
    ("B", 0, -1), ("B", 0, 1),
    ("A", 0, -1), ("A", 0, 1),
    ("B", -1, 0), ("B", 1, 0),
    ("A", 2, 0), ("A", 1, -1),
    ("A", 1, 1), ("B", -1, -1),
    ("A", -1, -1), ("A", -1, 1),
    ("B", 1, -1), ("B", -1, 1),
    ("B", 0, 2), ("B", 1, 1),
    ("A", 0, 2), ("B", 2, -1),
    ("B", 2, 0), ("A", 2, -1),
    ("A", 2, 1), ("B", -1, 2),
    ("A", 1, 2), ("A", -1, 2),
    ("B", 1, 2), ("B", 2, 2),
    ("B", 2, 1), ("A", 2, 2),
]
SLOT = {key: divmod(n, 2) for n, key in enumerate(ORDER)}
UNITS = 16
CHUNKS = 4
STAGES = ("gather", "product", "pair", "ring1", "ring2", "spread", "relay", "sibling", "final")
STEPS = [
    32, 64, 2, 3, 4, 33, 5, 34, 65, 96, 66, 8, 9, 6, 36, 7, 35, 68, 97, 128,
    67, 98, 10, 13, 11, 37, 12, 160, 38, 100, 69, 70, 99, 16, 17, 40, 15, 14, 129, 39,
    72, 192, 71, 132, 101, 102, 21, 20, 42, 19, 18, 41, 104, 74, 73, 103, 130, 133, 131, 161,
    23, 22, 164, 43, 134, 106, 105, 75, 25, 162, 193, 163, 26, 27, 45, 136, 24, 44, 30, 165,
    107, 77, 135, 28, 76, 31, 194, 224, 47, 138, 29, 46, 79, 78, 225, 109, 195, 197, 137, 139,
    108, 166, 110, 170, 226, 111, 141, 257, 167, 196, 171, 140, 169, 142, 198, 227, 143, 202, 256, 199,
    173, 258, 259, 168, 201, 172, 229, 230, 228, 174, 203, 231, 175, 260, 200, 233, 262, 234, 263, 204,
    205, 265, 206, 235, 261, 266, 207, 232, 267, 236, 237, 238, 264, 268, 239, 269, 270, 271,
]
LINKS = {"x+": (1, 0), "x-": (-1, 0), "y+": (0, 1), "y-": (0, -1)}


def forwards(half, dx, dy):
    out = []
    if half == "A":
        if dy == 0:
            if dx == 0:
                out += [("x-", ("A", 1, 0)), ("x+", ("A", -1, 0))]
            out += [("y+", ("A", dx, -1)), ("y-", ("A", dx, 1))]
            if dx == 1:
                out += [("x-", ("A", 2, 0))]
        elif dy == 1 and dx in (0, 1):
            out += [("y-", ("A", dx, 2))]
        elif dy == -1 and dx in (-1, 2):
            out += [("y+", ("A", dx, 2))]
    else:
        if dx == 0:
            if dy == 0:
                out += [("y+", ("B", 0, -1)), ("y-", ("B", 0, 1))]
            out += [("x+", ("B", -1, dy)), ("x-", ("B", 1, dy))]
            if dy == -1:
                out += [("y+", ("B", 0, 2))]
        elif dx == 1 and dy in (0, 1):
            out += [("x-", ("B", 2, dy))]
        elif dx == -1 and dy in (-1, 2):
            out += [("x+", ("B", 2, dy))]
    return out


def kernel(
    ints_hbm, mask_hbm, occ_hbm, virt_hbm, out_ref,
    masked, virt, occ, part, xr, sums, r1, s2, r2, fin, half, acc, mrow, mask_ref, occ_ref,
    load_sem, small_sem, virt_sem, occ_send, occ_recv, x_send, x_recv, r1_send, r1_recv, r2_send, r2_recv,
    a_send, a_recv, g1_send, g1_recv, g2_send, g2_recv, s_send, s_recv,
):
    mu, nu = lax.axis_index("mu"), lax.axis_index("nu")
    x, y, z, c = nu // 4, nu % 4, mu // 2, mu % 2
    rows, cols = ints_hbm.shape[1:]

    @functools.cache
    def at(dx=0, dy=0, dz=0, dc=0):
        return {
            "mu": ((z + dz + 4) % 4) * 2 + (c + dc) % 2,
            "nu": ((x + dx + 4) % 4) * 4 + (y + dy + 4) % 4,
        }

    def send(src, dst, send_sem, recv_sem, to):
        pltpu.make_async_remote_copy(
            src_ref=src, dst_ref=dst, send_sem=send_sem, recv_sem=recv_sem, device_id=to, device_id_type=MESH
        ).start()

    def wait(ref, sem):
        pltpu.make_async_copy(ref, ref, sem).wait()

    small = [
        pltpu.make_async_copy(occ_hbm, occ_ref, small_sem.at[0]),
        pltpu.make_async_copy(mask_hbm, mask_ref, small_sem.at[1]),
    ]
    chunk = rows // CHUNKS
    loads = [
        pltpu.make_async_copy(
            ints_hbm.at[p, pl.ds(q * chunk, chunk)],
            masked.at[pl.ds(q * chunk, chunk), pl.ds(p * cols, cols)],
            load_sem.at[q, p],
        )
        for q in range(CHUNKS)
        for p in range(2)
    ]

    barrier = pltpu.get_barrier_semaphore()
    greet = [at(*step) for step in LINKS.values()] + [at(dz=1), at(dz=-1), at(dc=1)]
    for to in greet:
        pl.semaphore_signal(barrier, inc=1, device_id=to, device_id_type=MESH)
    for load in small + loads:
        load.start()

    small[0].wait()
    occ[0] = occ_ref[...].T.reshape(2, BLK, rows)
    pl.semaphore_wait(barrier, len(greet))

    def occ_send_to(key, link, their):
        (u, h), (tu, th) = SLOT[key], SLOT[their]
        send(occ.at[u, h], occ.at[tu, th], occ_send, occ_recv.at[tu, th], at(*LINKS[link]))

    for link, key, their in [
        ("x-", ("A", 0, 0), ("A", 1, 0)), ("x+", ("A", 0, 0), ("A", -1, 0)),
        ("y+", ("B", 0, 0), ("B", 0, -1)), ("y-", ("B", 0, 0), ("B", 0, 1)),
        ("y+", ("A", 0, 0), ("A", 0, -1)), ("y-", ("A", 0, 0), ("A", 0, 1)),
        ("x+", ("B", 0, 0), ("B", -1, 0)), ("x-", ("B", 0, 0), ("B", 1, 0)),
    ]:
        occ_send_to(key, link, their)

    small[1].wait()
    n_blocks, m_blocks = mask_ref.shape
    lane_block = lax.broadcasted_iota(jnp.int32, (n_blocks, 2 * cols), 1) % cols // BLK
    pick = lane_block == lax.broadcasted_iota(jnp.int32, lane_block.shape, 0)
    mrow[...] = lax.dot_general(
        mask_ref[...].astype(BF16), pick.astype(BF16), (((0,), (0,)), ((), ())), preferred_element_type=F32
    )
    virt_load = pltpu.make_async_copy(virt_hbm, virt, virt_sem)
    virt_load.start()
    per = chunk // BLK
    for q in range(CHUNKS):
        for load in loads[2 * q : 2 * q + 2]:
            load.wait()
        for r in range(q * per, (q + 1) * per):
            keep = mrow[r : r + 1, :].astype(BF16)
            masked[r * BLK : (r + 1) * BLK, :] = masked[r * BLK : (r + 1) * BLK, :] * keep

    mine = pl.ds(pl.multiple_of(c * cols, 128), cols)
    theirs = pl.ds(pl.multiple_of((1 - c) * cols, 128), cols)
    mine_rows = pl.ds(pl.multiple_of(c * BLK, 16), BLK)
    their_rows = pl.ds(pl.multiple_of((1 - c) * BLK, 16), BLK)

    @functools.cache
    def zrows(dz):
        return pl.ds(pl.multiple_of(((z + dz + 4) % 4) * 16, 16), 16)

    @functools.cache
    def hrows(dz):
        return pl.ds(pl.multiple_of(c * BLK + ((z + dz + 4) % 4) * 16, 16), 16)

    def gather(n):
        u, h = divmod(n, 2)
        wait(occ.at[u, h], occ_recv.at[u, h])
        for link, their in forwards(*ORDER[n]):
            occ_send_to(ORDER[n], link, their)

    def product(u):
        left = occ[u].reshape(2 * BLK, rows)
        for j in range(0, 2 * cols, 256):
            tile = jnp.dot(left, masked[:, j : j + 256], preferred_element_type=F32)
            part[u, :, :, j : j + 256] = tile.astype(BF16).reshape(2, BLK, 256)
        send(part.at[u, :, :, theirs], xr.at[u], x_send, x_recv.at[u], at(dc=1))

    def pair(u):
        wait(xr.at[u], x_recv.at[u])
        sums[u] = (part[u, :, :, mine].astype(F32) + xr[u].astype(F32)).astype(BF16)
        send(sums.at[u, 0, zrows(2)], r1.at[u, 0], r1_send, r1_recv.at[u, 0], at(dz=1))
        send(sums.at[u, 1, zrows(2)], r1.at[u, 1], r1_send, r1_recv.at[u, 1], at(dz=-1))
        send(sums.at[u, 1, zrows(1)], r2.at[u, 0, 1], r2_send, r2_recv.at[u, 0], at(dz=1))
        send(sums.at[u, 0, zrows(-1)], r2.at[u, 1, 0], r2_send, r2_recv.at[u, 1], at(dz=-1))

    def ring1(u):
        for side, dz in ((0, 1), (1, -1)):
            wait(r1.at[u, side], r1_recv.at[u, side])
            own = sums[u, side, zrows(dz)].astype(F32)
            s2[u, side] = (own + r1[u, side].astype(F32)).astype(BF16)
            send(s2.at[u, side], r2.at[u, side, side], r2_send, r2_recv.at[u, side], at(dz=dz))

    def ring2(u):
        for side in range(2):
            wait(r2.at[u, side], r2_recv.at[u, side])
        total = sums[u, :, zrows(0)].astype(F32) + r2[u, 0].astype(F32) + r2[u, 1].astype(F32)
        if u == 0:
            half[0, :, hrows(0)] = total.astype(BF16)
            return
        fin[u] = total.astype(BF16)
        for h in range(2):
            _, dx, dy = ORDER[2 * u + h]
            send(fin.at[u, h], half.at[u, h, hrows(0)], a_send, a_recv.at[u], at(dx, dy))

    def spread(u):
        here = half.at[u, :, hrows(0)]
        if u > 0:
            wait(here, a_recv.at[u])
        send(here, here, g1_send, g1_recv.at[u, 0], at(dz=1))
        send(here, here, g1_send, g1_recv.at[u, 1], at(dz=-1))

    def relay(u):
        for side, dz in ((0, 1), (1, -1)):
            came = half.at[u, :, hrows(-dz)]
            wait(came, g1_recv.at[u, side])
            on = half.at[u, side, hrows(-dz)]
            send(on, on, g2_send, g2_recv.at[u, side], at(dz=dz))

    def sibling(u):
        for side in range(2):
            wait(half.at[u, side, hrows(2)], g2_recv.at[u, side])
        whole = half.at[u, :, mine_rows]
        send(whole, whole, s_send, s_recv.at[u], at(dc=1))

    started = []

    def final(u):
        wait(half.at[u, :, their_rows], s_recv.at[u])
        for h in range(2):
            kind, dx, dy = ORDER[2 * u + h]
            (ua, ha), (ub, hb) = SLOT["A", dx, dy], SLOT["B", dx, dy]
            if (u, h) != max((ua, ha), (ub, hb)):
                continue
            left = jnp.concatenate([half[ua, ha], half[ub, hb]], axis=0)
            n_block = ((x - dx + 4) % 4) * 4 + (y - dy + 4) % 4
            deep = pl.ds(pl.multiple_of(n_block * cols, cols), cols)
            for j in range(0, virt.shape[1], 256):
                term = jnp.dot(left, virt[deep, j : j + 256], preferred_element_type=F32)
                acc[:, j : j + 256] = acc[:, j : j + 256] + term if started else term
            started.append(u)

    stages = (gather, product, pair, ring1, ring2, spread, relay, sibling, final)
    need_virt = True
    for step in STEPS:
        stage, n = divmod(step, 32)
        if need_virt and STAGES[stage] == "final":
            virt_load.wait()
            need_virt = False
        stages[stage](n)

    out_ref[...] = acc[...].astype(BF16)
    wait(occ.at[pl.ds(1, UNITS - 1)], occ_send)
    wait(xr, x_send)
    wait(r1, r1_send)
    wait(r2, r2_send)
    wait(fin.at[pl.ds(1, UNITS - 1)], a_send)
    wait(r2, g1_send)
    wait(r1, g2_send)
    wait(xr, s_send)


def shards(integrals, block_mask, occ_coef, virt_coef):
    _, rows, cols = integrals.shape
    own, virt_cols = occ_coef.shape[1], virt_coef.shape[1]
    assert own == 2 * BLK
    vmem, dma = pltpu.VMEM, pltpu.SemaphoreType.DMA
    result = pl.pallas_call(
        kernel,
        name="transform",
        out_shape=jax.ShapeDtypeStruct((2 * own, virt_cols), BF16),
        in_specs=[
            pl.BlockSpec(memory_space=pl.ANY),
            pl.BlockSpec(memory_space=pl.ANY),
            pl.BlockSpec(memory_space=pl.ANY),
            pl.BlockSpec(memory_space=pl.ANY),
        ],
        out_specs=pl.BlockSpec(memory_space=pltpu.VMEM),
        scratch_shapes=[
            vmem((rows, 2 * cols), BF16),
            vmem(virt_coef.shape, BF16),
            vmem((UNITS, 2, BLK, rows), BF16),
            vmem((UNITS, 2, BLK, 2 * cols), BF16),
            vmem((UNITS, 2, BLK, cols), BF16),
            vmem((UNITS, 2, BLK, cols), BF16),
            vmem((UNITS, 2, 16, cols), BF16),
            vmem((UNITS, 2, 16, cols), BF16),
            vmem((UNITS, 2, 2, 16, cols), BF16),
            vmem((UNITS, 2, 16, cols), BF16),
            vmem((UNITS, 2, 2 * BLK, cols), BF16),
            vmem((2 * own, virt_cols), F32),
            vmem((block_mask.shape[0], 2 * cols), F32),
            vmem(block_mask.shape[::-1], jnp.int32),
            vmem(occ_coef.shape, BF16),
            dma((CHUNKS, 2)), dma((2,)), dma,
            dma, dma((UNITS, 2)),
            dma, dma((UNITS,)),
            dma, dma((UNITS, 2)),
            dma, dma((UNITS, 2)),
            dma, dma((UNITS,)),
            dma, dma((UNITS, 2)),
            dma, dma((UNITS, 2)),
            dma, dma((UNITS,)),
        ],
        compiler_params=pltpu.CompilerParams(
            collective_id=0, has_side_effects=True, vmem_limit_bytes=62 * 2**20
        ),
    )(integrals, block_mask.T, occ_coef, virt_coef)
    result = result.reshape(2, 2, BLK, virt_cols).transpose(0, 2, 1, 3)
    return result.reshape(own, 2, virt_cols)


def solution(mesh):
    return jax.shard_map(
        shards,
        mesh=mesh,
        in_specs=(P(None, "mu", "nu"), P("mu", "nu"), P("mu", "nu"), P(None, "mu")),
        out_specs=P("nu", None, "mu"),
        check_vma=False,
    )
```

```python
import functools

import jax
import jax.numpy as jnp
from jax import lax
from jax.experimental import pallas as pl
from jax.experimental.pallas import tpu as pltpu
from jax.sharding import PartitionSpec as P

MESH = pl.DeviceIdType.MESH
BLK = 64
F32, BF16 = jnp.float32, jnp.bfloat16

ORDER = [
    ("A", 0, 0), ("B", 0, 0),
    ("A", 1, 0), ("A", -1, 0),
    ("B", 0, -1), ("B", 0, 1),
    ("A", 0, -1), ("A", 0, 1),
    ("B", -1, 0), ("B", 1, 0),
    ("A", 2, 0), ("A", 1, -1),
    ("A", 1, 1), ("B", -1, -1),
    ("A", -1, -1), ("A", -1, 1),
    ("B", 1, -1), ("B", -1, 1),
    ("B", 0, 2), ("B", 1, 1),
    ("A", 0, 2), ("B", 2, -1),
    ("B", 2, 0), ("A", 2, -1),
    ("A", 2, 1), ("B", -1, 2),
    ("A", 1, 2), ("A", -1, 2),
    ("B", 1, 2), ("B", 2, 2),
    ("B", 2, 1), ("A", 2, 2),
]
SLOT = {key: divmod(n, 2) for n, key in enumerate(ORDER)}
UNITS = 16
CHUNKS = 4
STAGES = ("gather", "product", "pair", "ring1", "ring2", "spread", "relay", "sibling", "final")
STEPS = [
    32, 64, 2, 3, 4, 33, 5, 34, 65, 96, 66, 8, 9, 6, 36, 7, 35, 68, 97, 128,
    67, 98, 10, 13, 11, 37, 12, 160, 38, 100, 69, 70, 99, 16, 17, 40, 15, 14, 129, 39,
    72, 192, 71, 132, 101, 102, 21, 20, 42, 19, 18, 41, 104, 74, 73, 103, 130, 133, 131, 161,
    23, 22, 164, 43, 134, 106, 105, 75, 25, 162, 193, 163, 26, 27, 45, 136, 24, 44, 30, 165,
    107, 77, 135, 28, 76, 31, 194, 224, 47, 138, 29, 46, 79, 78, 225, 109, 195, 197, 137, 139,
    108, 166, 110, 170, 226, 111, 141, 257, 167, 196, 171, 140, 169, 142, 198, 227, 143, 202, 256, 199,
    173, 258, 259, 168, 201, 172, 229, 230, 228, 174, 203, 231, 175, 260, 200, 233, 262, 234, 263, 204,
    205, 265, 206, 235, 261, 266, 207, 232, 267, 236, 237, 238, 264, 268, 239, 269, 270, 271,
]
LINKS = {"x+": (1, 0), "x-": (-1, 0), "y+": (0, 1), "y-": (0, -1)}


def forwards(half, dx, dy):
    out = []
    if half == "A":
        if dy == 0:
            if dx == 0:
                out += [("x-", ("A", 1, 0)), ("x+", ("A", -1, 0))]
            out += [("y+", ("A", dx, -1)), ("y-", ("A", dx, 1))]
            if dx == 1:
                out += [("x-", ("A", 2, 0))]
        elif dy == 1 and dx in (0, 1):
            out += [("y-", ("A", dx, 2))]
        elif dy == -1 and dx in (-1, 2):
            out += [("y+", ("A", dx, 2))]
    else:
        if dx == 0:
            if dy == 0:
                out += [("y+", ("B", 0, -1)), ("y-", ("B", 0, 1))]
            out += [("x+", ("B", -1, dy)), ("x-", ("B", 1, dy))]
            if dy == -1:
                out += [("y+", ("B", 0, 2))]
        elif dx == 1 and dy in (0, 1):
            out += [("x-", ("B", 2, dy))]
        elif dx == -1 and dy in (-1, 2):
            out += [("x+", ("B", 2, dy))]
    return out


def kernel(
    ints_hbm, mask_hbm, occ_hbm, virt_hbm, out_ref,
    masked, virt, occ, part, xr, sums, r1, s2, r2, fin, half, acc, mrow, mask_ref, occ_ref,
    load_sem, small_sem, virt_sem, occ_send, occ_recv, x_send, x_recv, r1_send, r1_recv, r2_send, r2_recv,
    a_send, a_recv, g1_send, g1_recv, g2_send, g2_recv, s_send, s_recv,
):
    mu, nu = lax.axis_index("mu"), lax.axis_index("nu")
    x, y, z, c = nu // 4, nu % 4, mu // 2, mu % 2
    rows, cols = ints_hbm.shape[1:]

    @functools.cache
    def at(dx=0, dy=0, dz=0, dc=0):
        return {
            "mu": ((z + dz + 4) % 4) * 2 + (c + dc) % 2,
            "nu": ((x + dx + 4) % 4) * 4 + (y + dy + 4) % 4,
        }

    def send(src, dst, send_sem, recv_sem, to):
        pltpu.make_async_remote_copy(
            src_ref=src, dst_ref=dst, send_sem=send_sem, recv_sem=recv_sem, device_id=to, device_id_type=MESH
        ).start()

    def wait(ref, sem):
        pltpu.make_async_copy(ref, ref, sem).wait()

    small = [
        pltpu.make_async_copy(occ_hbm, occ_ref, small_sem.at[0]),
        pltpu.make_async_copy(mask_hbm, mask_ref, small_sem.at[1]),
    ]
    chunk = rows // CHUNKS
    loads = [
        pltpu.make_async_copy(
            ints_hbm.at[p, pl.ds(q * chunk, chunk)],
            masked.at[pl.ds(q * chunk, chunk), pl.ds(p * cols, cols)],
            load_sem.at[q, p],
        )
        for q in range(CHUNKS)
        for p in range(2)
    ]

    barrier = pltpu.get_barrier_semaphore()
    greet = [at(*step) for step in LINKS.values()] + [at(dz=1), at(dz=-1), at(dc=1)]
    for to in greet:
        pl.semaphore_signal(barrier, inc=1, device_id=to, device_id_type=MESH)
    for load in small + loads:
        load.start()

    small[0].wait()
    occ[0] = occ_ref[...].T.reshape(2, BLK, rows)
    pl.semaphore_wait(barrier, len(greet))

    def occ_send_to(key, link, their):
        (u, h), (tu, th) = SLOT[key], SLOT[their]
        for low in range(0, BLK, 32):
            rows_at = pl.ds(low, 32)
            send(occ.at[u, h, rows_at], occ.at[tu, th, rows_at], occ_send, occ_recv.at[tu, th], at(*LINKS[link]))

    for link, key, their in [
        ("x-", ("A", 0, 0), ("A", 1, 0)), ("x+", ("A", 0, 0), ("A", -1, 0)),
        ("y+", ("B", 0, 0), ("B", 0, -1)), ("y-", ("B", 0, 0), ("B", 0, 1)),
        ("y+", ("A", 0, 0), ("A", 0, -1)), ("y-", ("A", 0, 0), ("A", 0, 1)),
        ("x+", ("B", 0, 0), ("B", -1, 0)), ("x-", ("B", 0, 0), ("B", 1, 0)),
    ]:
        occ_send_to(key, link, their)

    small[1].wait()
    n_blocks, m_blocks = mask_ref.shape
    lane_block = lax.broadcasted_iota(jnp.int32, (n_blocks, 2 * cols), 1) % cols // BLK
    pick = lane_block == lax.broadcasted_iota(jnp.int32, lane_block.shape, 0)
    mrow[...] = lax.dot_general(
        mask_ref[...].astype(BF16), pick.astype(BF16), (((0,), (0,)), ((), ())), preferred_element_type=F32
    )
    virt_load = pltpu.make_async_copy(virt_hbm, virt, virt_sem)
    virt_load.start()
    per = chunk // BLK
    for q in range(CHUNKS):
        for load in loads[2 * q : 2 * q + 2]:
            load.wait()
        for r in range(q * per, (q + 1) * per):
            keep = mrow[r : r + 1, :].astype(BF16)
            masked[r * BLK : (r + 1) * BLK, :] = masked[r * BLK : (r + 1) * BLK, :] * keep

    mine = pl.ds(pl.multiple_of(c * cols, 128), cols)
    theirs = pl.ds(pl.multiple_of((1 - c) * cols, 128), cols)
    mine_rows = pl.ds(pl.multiple_of(c * BLK, 16), BLK)
    their_rows = pl.ds(pl.multiple_of((1 - c) * BLK, 16), BLK)

    @functools.cache
    def zrows(dz):
        return pl.ds(pl.multiple_of(((z + dz + 4) % 4) * 16, 16), 16)

    @functools.cache
    def hrows(dz):
        return pl.ds(pl.multiple_of(c * BLK + ((z + dz + 4) % 4) * 16, 16), 16)

    def gather(n):
        u, h = divmod(n, 2)
        wait(occ.at[u, h], occ_recv.at[u, h])
        for link, their in forwards(*ORDER[n]):
            occ_send_to(ORDER[n], link, their)

    def product(u):
        left = occ[u].reshape(2 * BLK, rows)
        for j in range(0, 2 * cols, 256):
            tile = jnp.dot(left, masked[:, j : j + 256], preferred_element_type=F32)
            part[u, :, :, j : j + 256] = tile.astype(BF16).reshape(2, BLK, 256)
        send(part.at[u, :, :, theirs], xr.at[u], x_send, x_recv.at[u], at(dc=1))

    def pair(u):
        wait(xr.at[u], x_recv.at[u])
        sums[u] = (part[u, :, :, mine].astype(F32) + xr[u].astype(F32)).astype(BF16)
        send(sums.at[u, 0, zrows(2)], r1.at[u, 0], r1_send, r1_recv.at[u, 0], at(dz=1))
        send(sums.at[u, 1, zrows(2)], r1.at[u, 1], r1_send, r1_recv.at[u, 1], at(dz=-1))
        send(sums.at[u, 1, zrows(1)], r2.at[u, 0, 1], r2_send, r2_recv.at[u, 0], at(dz=1))
        send(sums.at[u, 0, zrows(-1)], r2.at[u, 1, 0], r2_send, r2_recv.at[u, 1], at(dz=-1))

    def ring1(u):
        for side, dz in ((0, 1), (1, -1)):
            wait(r1.at[u, side], r1_recv.at[u, side])
            own = sums[u, side, zrows(dz)].astype(F32)
            s2[u, side] = (own + r1[u, side].astype(F32)).astype(BF16)
            send(s2.at[u, side], r2.at[u, side, side], r2_send, r2_recv.at[u, side], at(dz=dz))

    def ring2(u):
        for side in range(2):
            wait(r2.at[u, side], r2_recv.at[u, side])
        total = sums[u, :, zrows(0)].astype(F32) + r2[u, 0].astype(F32) + r2[u, 1].astype(F32)
        if u == 0:
            half[0, :, hrows(0)] = total.astype(BF16)
            return
        fin[u] = total.astype(BF16)
        for h in range(2):
            _, dx, dy = ORDER[2 * u + h]
            send(fin.at[u, h], half.at[u, h, hrows(0)], a_send, a_recv.at[u], at(dx, dy))

    def spread(u):
        here = half.at[u, :, hrows(0)]
        if u > 0:
            wait(here, a_recv.at[u])
        send(here, here, g1_send, g1_recv.at[u, 0], at(dz=1))
        send(here, here, g1_send, g1_recv.at[u, 1], at(dz=-1))

    def relay(u):
        for side, dz in ((0, 1), (1, -1)):
            came = half.at[u, :, hrows(-dz)]
            wait(came, g1_recv.at[u, side])
            on = half.at[u, side, hrows(-dz)]
            send(on, on, g2_send, g2_recv.at[u, side], at(dz=dz))

    def sibling(u):
        for side in range(2):
            wait(half.at[u, side, hrows(2)], g2_recv.at[u, side])
        whole = half.at[u, :, mine_rows]
        send(whole, whole, s_send, s_recv.at[u], at(dc=1))

    started = []

    def final(u):
        wait(half.at[u, :, their_rows], s_recv.at[u])
        for h in range(2):
            kind, dx, dy = ORDER[2 * u + h]
            (ua, ha), (ub, hb) = SLOT["A", dx, dy], SLOT["B", dx, dy]
            if (u, h) != max((ua, ha), (ub, hb)):
                continue
            left = jnp.concatenate([half[ua, ha], half[ub, hb]], axis=0)
            n_block = ((x - dx + 4) % 4) * 4 + (y - dy + 4) % 4
            deep = pl.ds(pl.multiple_of(n_block * cols, cols), cols)
            for j in range(0, virt.shape[1], 256):
                term = jnp.dot(left, virt[deep, j : j + 256], preferred_element_type=F32)
                acc[:, j : j + 256] = acc[:, j : j + 256] + term if started else term
            started.append(u)

    stages = (gather, product, pair, ring1, ring2, spread, relay, sibling, final)
    need_virt = True
    for step in STEPS:
        stage, n = divmod(step, 32)
        if need_virt and STAGES[stage] == "final":
            virt_load.wait()
            need_virt = False
        stages[stage](n)

    n_rows = out_ref.shape[0]
    to_row = lax.broadcasted_iota(jnp.int32, (n_rows, n_rows), 0)
    from_row = lax.broadcasted_iota(jnp.int32, (n_rows, n_rows), 1)
    pair_row = to_row % (2 * BLK)
    swap = (from_row == to_row - pair_row + pair_row % 2 * BLK + pair_row // 2).astype(BF16)
    for j in range(0, out_ref.shape[1], 256):
        rounded = acc[:, j : j + 256].astype(BF16)
        out_ref[:, j : j + 256] = jnp.dot(swap, rounded, preferred_element_type=F32).astype(BF16)
    wait(occ.at[pl.ds(1, UNITS - 1)], occ_send)
    wait(xr, x_send)
    wait(r1, r1_send)
    wait(r2, r2_send)
    wait(fin.at[pl.ds(1, UNITS - 1)], a_send)
    wait(r2, g1_send)
    wait(r1, g2_send)
    wait(xr, s_send)


def shards(integrals, block_mask, occ_coef, virt_coef):
    _, rows, cols = integrals.shape
    own, virt_cols = occ_coef.shape[1], virt_coef.shape[1]
    assert own == 2 * BLK
    vmem, dma = pltpu.VMEM, pltpu.SemaphoreType.DMA
    result = pl.pallas_call(
        kernel,
        name="transform",
        out_shape=jax.ShapeDtypeStruct((2 * own, virt_cols), BF16),
        in_specs=[
            pl.BlockSpec(memory_space=pl.ANY),
            pl.BlockSpec(memory_space=pl.ANY),
            pl.BlockSpec(memory_space=pl.ANY),
            pl.BlockSpec(memory_space=pl.ANY),
        ],
        out_specs=pl.BlockSpec(memory_space=pltpu.VMEM),
        scratch_shapes=[
            vmem((rows, 2 * cols), BF16),
            vmem(virt_coef.shape, BF16),
            vmem((UNITS, 2, BLK, rows), BF16),
            vmem((UNITS, 2, BLK, 2 * cols), BF16),
            vmem((UNITS, 2, BLK, cols), BF16),
            vmem((UNITS, 2, BLK, cols), BF16),
            vmem((UNITS, 2, 16, cols), BF16),
            vmem((UNITS, 2, 16, cols), BF16),
            vmem((UNITS, 2, 2, 16, cols), BF16),
            vmem((UNITS, 2, 16, cols), BF16),
            vmem((UNITS, 2, 2 * BLK, cols), BF16),
            vmem((2 * own, virt_cols), F32),
            vmem((block_mask.shape[0], 2 * cols), F32),
            vmem(block_mask.shape[::-1], jnp.int32),
            vmem(occ_coef.shape, BF16),
            dma((CHUNKS, 2)), dma((2,)), dma,
            dma, dma((UNITS, 2)),
            dma, dma((UNITS,)),
            dma, dma((UNITS, 2)),
            dma, dma((UNITS, 2)),
            dma, dma((UNITS,)),
            dma, dma((UNITS, 2)),
            dma, dma((UNITS, 2)),
            dma, dma((UNITS,)),
        ],
        compiler_params=pltpu.CompilerParams(
            collective_id=0, has_side_effects=True, vmem_limit_bytes=62 * 2**20
        ),
    )(integrals, block_mask.T, occ_coef, virt_coef)
    return result.reshape(own, 2, virt_cols)


def solution(mesh):
    return jax.shard_map(
        shards,
        mesh=mesh,
        in_specs=(P(None, "mu", "nu"), P("mu", "nu"), P("mu", "nu"), P(None, "mu")),
        out_specs=P("nu", None, "mu"),
        check_vma=False,
    )
```

```python
import functools

import jax
import jax.numpy as jnp
from jax import lax
from jax.experimental import pallas as pl
from jax.experimental.pallas import tpu as pltpu
from jax.sharding import PartitionSpec as P

MESH = pl.DeviceIdType.MESH
BLK = 64
F32, BF16 = jnp.float32, jnp.bfloat16

ORDER = [
    ("A", 0, 0), ("B", 0, 0),
    ("A", 1, 0), ("A", -1, 0),
    ("B", 0, -1), ("B", 0, 1),
    ("A", 0, -1), ("A", 0, 1),
    ("B", -1, 0), ("B", 1, 0),
    ("A", 2, 0), ("A", 1, -1),
    ("A", 1, 1), ("B", -1, -1),
    ("A", -1, -1), ("A", -1, 1),
    ("B", 1, -1), ("B", -1, 1),
    ("B", 0, 2), ("B", 1, 1),
    ("A", 0, 2), ("B", 2, -1),
    ("B", 2, 0), ("A", 2, -1),
    ("A", 2, 1), ("B", -1, 2),
    ("A", 1, 2), ("A", -1, 2),
    ("B", 1, 2), ("B", 2, 2),
    ("B", 2, 1), ("A", 2, 2),
]
SLOT = {key: divmod(n, 2) for n, key in enumerate(ORDER)}
UNITS = 16
CHUNKS = 4
DIRECT = range(5)
STAGES = ("gather", "product", "pair", "ring1", "ring2", "spread", "relay", "sibling", "final")
STEPS = [
    32, 64, 2, 4, 5, 34, 3, 66, 33, 97, 7, 6, 65, 8, 9, 128, 35, 160, 36, 68,
    13, 11, 130, 12, 38, 10, 37, 70, 129, 67, 18, 16, 17, 40, 69, 192, 132, 72, 102, 15,
    14, 39, 162, 100, 21, 20, 19, 42, 71, 131, 74, 104, 224, 101, 41, 134, 161, 194, 22, 73,
    103, 23, 25, 43, 106, 75, 27, 26, 193, 96, 24, 28, 163, 133, 44, 164, 45, 105, 77, 226,
    107, 30, 76, 31, 135, 47, 29, 46, 195, 79, 78, 136, 196, 138, 137, 108, 109, 139, 167, 166,
    110, 111, 169, 227, 141, 170, 225, 228, 171, 140, 168, 165, 199, 258, 142, 259, 198, 99, 143, 173,
    203, 202, 256, 257, 201, 172, 174, 231, 197, 230, 260, 262, 175, 233, 235, 200, 263, 205, 204, 234,
    265, 206, 229, 266, 207, 98, 261, 232, 267, 236, 237, 238, 264, 268, 239, 269, 270, 271,
]
LINKS = {"x+": (1, 0), "x-": (-1, 0), "y+": (0, 1), "y-": (0, -1)}


def forwards(half, dx, dy):
    out = []
    if half == "A":
        if dy == 0:
            if dx == 0:
                out += [("x-", ("A", 1, 0)), ("x+", ("A", -1, 0))]
            out += [("y+", ("A", dx, -1)), ("y-", ("A", dx, 1))]
            if dx == 1:
                out += [("x-", ("A", 2, 0))]
        elif dy == 1 and dx in (0, 1):
            out += [("y-", ("A", dx, 2))]
        elif dy == -1 and dx in (-1, 2):
            out += [("y+", ("A", dx, 2))]
    else:
        if dx == 0:
            if dy == 0:
                out += [("y+", ("B", 0, -1)), ("y-", ("B", 0, 1))]
            out += [("x+", ("B", -1, dy)), ("x-", ("B", 1, dy))]
            if dy == -1:
                out += [("y+", ("B", 0, 2))]
        elif dx == 1 and dy in (0, 1):
            out += [("x-", ("B", 2, dy))]
        elif dx == -1 and dy in (-1, 2):
            out += [("x+", ("B", 2, dy))]
    return out


def kernel(
    ints_hbm, mask_hbm, occ_hbm, virt_hbm, out_ref,
    masked, virt, occ, part, xr, sums, r1, s2, r2, fin, half, acc, mrow, mask_ref, occ_ref,
    load_sem, small_sem, virt_sem, occ_send, occ_recv, x_send, x_recv, r1_send, r1_recv, r2_send, r2_recv,
    a_send, a_recv, g1_send, g1_recv, g2_send, g2_recv, s_send, s_recv,
):
    mu, nu = lax.axis_index("mu"), lax.axis_index("nu")
    x, y, z, c = nu // 4, nu % 4, mu // 2, mu % 2
    rows, cols = ints_hbm.shape[1:]

    @functools.cache
    def at(dx=0, dy=0, dz=0, dc=0):
        return {
            "mu": ((z + dz + 4) % 4) * 2 + (c + dc) % 2,
            "nu": ((x + dx + 4) % 4) * 4 + (y + dy + 4) % 4,
        }

    def send(src, dst, send_sem, recv_sem, to):
        pltpu.make_async_remote_copy(
            src_ref=src, dst_ref=dst, send_sem=send_sem, recv_sem=recv_sem, device_id=to, device_id_type=MESH
        ).start()

    def wait(ref, sem):
        pltpu.make_async_copy(ref, ref, sem).wait()

    small = [
        pltpu.make_async_copy(occ_hbm, occ_ref, small_sem.at[0]),
        pltpu.make_async_copy(mask_hbm, mask_ref, small_sem.at[1]),
    ]
    chunk = rows // CHUNKS
    loads = [
        pltpu.make_async_copy(
            ints_hbm.at[p, pl.ds(q * chunk, chunk)],
            masked.at[pl.ds(q * chunk, chunk), pl.ds(p * cols, cols)],
            load_sem.at[q, p],
        )
        for q in range(CHUNKS)
        for p in range(2)
    ]

    barrier = pltpu.get_barrier_semaphore()
    greet = [at(*step) for step in LINKS.values()] + [at(dz=1), at(dz=-1), at(dz=2), at(dc=1)]
    for to in greet:
        pl.semaphore_signal(barrier, inc=1, device_id=to, device_id_type=MESH)
    for load in small + loads:
        load.start()

    small[0].wait()
    occ[0] = occ_ref[...].T.reshape(2, BLK, rows)
    pl.semaphore_wait(barrier, len(greet))

    def occ_send_to(key, link, their):
        (u, h), (tu, th) = SLOT[key], SLOT[their]
        send(occ.at[u, h], occ.at[tu, th], occ_send, occ_recv.at[tu, th], at(*LINKS[link]))

    for link, key, their in [
        ("x-", ("A", 0, 0), ("A", 1, 0)), ("x+", ("A", 0, 0), ("A", -1, 0)),
        ("y+", ("B", 0, 0), ("B", 0, -1)), ("y-", ("B", 0, 0), ("B", 0, 1)),
        ("y+", ("A", 0, 0), ("A", 0, -1)), ("y-", ("A", 0, 0), ("A", 0, 1)),
        ("x+", ("B", 0, 0), ("B", -1, 0)), ("x-", ("B", 0, 0), ("B", 1, 0)),
    ]:
        occ_send_to(key, link, their)

    small[1].wait()
    n_blocks, m_blocks = mask_ref.shape
    lane_block = lax.broadcasted_iota(jnp.int32, (n_blocks, 2 * cols), 1) % cols // BLK
    pick = lane_block == lax.broadcasted_iota(jnp.int32, lane_block.shape, 0)
    mrow[...] = lax.dot_general(
        mask_ref[...].astype(BF16), pick.astype(BF16), (((0,), (0,)), ((), ())), preferred_element_type=F32
    )
    virt_load = pltpu.make_async_copy(virt_hbm, virt, virt_sem)
    virt_load.start()
    per = chunk // BLK
    for q in range(CHUNKS):
        for load in loads[2 * q : 2 * q + 2]:
            load.wait()
        for r in range(q * per, (q + 1) * per):
            keep = mrow[r : r + 1, :].astype(BF16)
            masked[r * BLK : (r + 1) * BLK, :] = masked[r * BLK : (r + 1) * BLK, :] * keep

    mine = pl.ds(pl.multiple_of(c * cols, 128), cols)
    theirs = pl.ds(pl.multiple_of((1 - c) * cols, 128), cols)
    mine_rows = pl.ds(pl.multiple_of(c * BLK, 16), BLK)
    their_rows = pl.ds(pl.multiple_of((1 - c) * BLK, 16), BLK)

    @functools.cache
    def zrows(dz):
        return pl.ds(pl.multiple_of(((z + dz + 4) % 4) * 16, 16), 16)

    @functools.cache
    def hrows(dz):
        return pl.ds(pl.multiple_of(c * BLK + ((z + dz + 4) % 4) * 16, 16), 16)

    def gather(n):
        u, h = divmod(n, 2)
        wait(occ.at[u, h], occ_recv.at[u, h])
        for link, their in forwards(*ORDER[n]):
            occ_send_to(ORDER[n], link, their)

    def product(u):
        left = occ[u].reshape(2 * BLK, rows)
        for j in range(0, 2 * cols, 256):
            tile = jnp.dot(left, masked[:, j : j + 256], preferred_element_type=F32)
            part[u, :, :, j : j + 256] = tile.astype(BF16).reshape(2, BLK, 256)
        send(part.at[u, :, :, theirs], xr.at[u], x_send, x_recv.at[u], at(dc=1))

    def pair(u):
        wait(xr.at[u], x_recv.at[u])
        sums[u] = (part[u, :, :, mine].astype(F32) + xr[u].astype(F32)).astype(BF16)
        if u in DIRECT:
            send(sums.at[u, :, zrows(1)], r2.at[u, 0], r2_send, r2_recv.at[u, 0], at(dz=1))
            send(sums.at[u, :, zrows(-1)], r2.at[u, 1], r2_send, r2_recv.at[u, 1], at(dz=-1))
            send(sums.at[u, :, zrows(2)], r1.at[u], r1_send, r1_recv.at[u, 0], at(dz=2))
            return
        send(sums.at[u, 0, zrows(2)], r1.at[u, 0], r1_send, r1_recv.at[u, 0], at(dz=1))
        send(sums.at[u, 1, zrows(2)], r1.at[u, 1], r1_send, r1_recv.at[u, 1], at(dz=-1))
        send(sums.at[u, 1, zrows(1)], r2.at[u, 0, 1], r2_send, r2_recv.at[u, 0], at(dz=1))
        send(sums.at[u, 0, zrows(-1)], r2.at[u, 1, 0], r2_send, r2_recv.at[u, 1], at(dz=-1))

    def ring1(u):
        if u in DIRECT:
            return
        for side, dz in ((0, 1), (1, -1)):
            wait(r1.at[u, side], r1_recv.at[u, side])
            own = sums[u, side, zrows(dz)].astype(F32)
            s2[u, side] = (own + r1[u, side].astype(F32)).astype(BF16)
            send(s2.at[u, side], r2.at[u, side, side], r2_send, r2_recv.at[u, side], at(dz=dz))

    def ring2(u):
        for side in range(2):
            wait(r2.at[u, side], r2_recv.at[u, side])
        total = sums[u, :, zrows(0)].astype(F32) + r2[u, 0].astype(F32) + r2[u, 1].astype(F32)
        if u in DIRECT:
            wait(r1.at[u], r1_recv.at[u, 0])
            total += r1[u].astype(F32)
        if u == 0:
            half[0, :, hrows(0)] = total.astype(BF16)
            return
        fin[u] = total.astype(BF16)
        for h in range(2):
            _, dx, dy = ORDER[2 * u + h]
            send(fin.at[u, h], half.at[u, h, hrows(0)], a_send, a_recv.at[u], at(dx, dy))

    def spread(u):
        here = half.at[u, :, hrows(0)]
        if u > 0:
            wait(here, a_recv.at[u])
        send(here, here, g1_send, g1_recv.at[u, 0], at(dz=1))
        send(here, here, g1_send, g1_recv.at[u, 1], at(dz=-1))

    def relay(u):
        for side, dz in ((0, 1), (1, -1)):
            came = half.at[u, :, hrows(-dz)]
            wait(came, g1_recv.at[u, side])
            on = half.at[u, side, hrows(-dz)]
            send(on, on, g2_send, g2_recv.at[u, side], at(dz=dz))

    def sibling(u):
        for side in range(2):
            wait(half.at[u, side, hrows(2)], g2_recv.at[u, side])
        whole = half.at[u, :, mine_rows]
        send(whole, whole, s_send, s_recv.at[u], at(dc=1))

    started = []

    def final(u):
        wait(half.at[u, :, their_rows], s_recv.at[u])
        for h in range(2):
            kind, dx, dy = ORDER[2 * u + h]
            (ua, ha), (ub, hb) = SLOT["A", dx, dy], SLOT["B", dx, dy]
            if (u, h) != max((ua, ha), (ub, hb)):
                continue
            left = jnp.concatenate([half[ua, ha], half[ub, hb]], axis=0)
            n_block = ((x - dx + 4) % 4) * 4 + (y - dy + 4) % 4
            deep = pl.ds(pl.multiple_of(n_block * cols, cols), cols)
            for j in range(0, virt.shape[1], 256):
                term = jnp.dot(left, virt[deep, j : j + 256], preferred_element_type=F32)
                acc[:, j : j + 256] = acc[:, j : j + 256] + term if started else term
            started.append(u)

    stages = (gather, product, pair, ring1, ring2, spread, relay, sibling, final)
    need_virt = True
    for step in STEPS:
        stage, n = divmod(step, 32)
        if need_virt and STAGES[stage] == "final":
            virt_load.wait()
            need_virt = False
        stages[stage](n)

    out_ref[...] = acc[...].astype(BF16)
    wait(occ.at[pl.ds(1, UNITS - 1)], occ_send)
    wait(xr, x_send)
    wait(r1, r1_send)
    wait(r2, r2_send)
    wait(fin.at[pl.ds(1, UNITS - 1)], a_send)
    wait(r2, g1_send)
    wait(r1, g2_send)
    wait(xr, s_send)


def shards(integrals, block_mask, occ_coef, virt_coef):
    _, rows, cols = integrals.shape
    own, virt_cols = occ_coef.shape[1], virt_coef.shape[1]
    assert own == 2 * BLK
    vmem, dma = pltpu.VMEM, pltpu.SemaphoreType.DMA
    result = pl.pallas_call(
        kernel,
        name="transform",
        out_shape=jax.ShapeDtypeStruct((2 * own, virt_cols), BF16),
        in_specs=[
            pl.BlockSpec(memory_space=pl.ANY),
            pl.BlockSpec(memory_space=pl.ANY),
            pl.BlockSpec(memory_space=pl.ANY),
            pl.BlockSpec(memory_space=pl.ANY),
        ],
        out_specs=pl.BlockSpec(memory_space=pltpu.VMEM),
        scratch_shapes=[
            vmem((rows, 2 * cols), BF16),
            vmem(virt_coef.shape, BF16),
            vmem((UNITS, 2, BLK, rows), BF16),
            vmem((UNITS, 2, BLK, 2 * cols), BF16),
            vmem((UNITS, 2, BLK, cols), BF16),
            vmem((UNITS, 2, BLK, cols), BF16),
            vmem((UNITS, 2, 16, cols), BF16),
            vmem((UNITS, 2, 16, cols), BF16),
            vmem((UNITS, 2, 2, 16, cols), BF16),
            vmem((UNITS, 2, 16, cols), BF16),
            vmem((UNITS, 2, 2 * BLK, cols), BF16),
            vmem((2 * own, virt_cols), F32),
            vmem((block_mask.shape[0], 2 * cols), F32),
            vmem(block_mask.shape[::-1], jnp.int32),
            vmem(occ_coef.shape, BF16),
            dma((CHUNKS, 2)), dma((2,)), dma,
            dma, dma((UNITS, 2)),
            dma, dma((UNITS,)),
            dma, dma((UNITS, 2)),
            dma, dma((UNITS, 2)),
            dma, dma((UNITS,)),
            dma, dma((UNITS, 2)),
            dma, dma((UNITS, 2)),
            dma, dma((UNITS,)),
        ],
        compiler_params=pltpu.CompilerParams(
            collective_id=0, has_side_effects=True, vmem_limit_bytes=62 * 2**20
        ),
    )(integrals, block_mask.T, occ_coef, virt_coef)
    result = result.reshape(2, 2, BLK, virt_cols).transpose(0, 2, 1, 3)
    return result.reshape(own, 2, virt_cols)


def solution(mesh):
    return jax.shard_map(
        shards,
        mesh=mesh,
        in_specs=(P(None, "mu", "nu"), P("mu", "nu"), P("mu", "nu"), P(None, "mu")),
        out_specs=P("nu", None, "mu"),
        check_vma=False,
    )
```
